32 devices in a mesh: replica: 4 (over z), fsdp: 8 (over y, x, core).
Axes of the slice: x: 2, y: 2, z: 4, core: 2. Of those that a mesh axis runs over, the one named last changes fastest.
Arguments:
- tokens: bfloat16 [8192, 768], P(('replica', 'fsdp')), may hold values from -6 to 6
- seq_lengths: int32 [32, 2], P(('replica', 'fsdp')), may hold values from 1 to 255, as said below
- norm1_gain: bfloat16 [768], P('fsdp'), may hold values from 0.5 to 1.5
- qkv_weight: bfloat16 [768, 2304], P('fsdp'), may hold values from -0.21875 to 0.21875
- out_weight: bfloat16 [768, 768], P('fsdp'), may hold values from -0.875 to 0.875
- norm2_gain: bfloat16 [768], P('fsdp'), may hold values from 0.5 to 1.5
- in_weight: bfloat16 [768, 2304], P('fsdp'), may hold values from -0.21875 to 0.21875
- down_weight: bfloat16 [1152, 768], P(None, 'fsdp'), may hold values from -0.1875 to 0.1875
- cotangent: float32 [8192, 768], P(('replica', 'fsdp')), may hold values from -6 to 6
Outputs:
- output: bfloat16 [8192, 768], P(('replica', 'fsdp'))
- grad_tokens: float32 [8192, 768], P(('replica', 'fsdp'))
- grad_norm1: float32 [768], P('fsdp')
- grad_qkv: float32 [768, 2304], P('fsdp')
- grad_out: float32 [768, 768], P('fsdp')
- grad_norm2: float32 [768], P('fsdp')
- grad_in: float32 [768, 2304], P('fsdp')
- grad_down: float32 [1152, 768], P(None, 'fsdp')
The draws below stay inside these ranges and needn't reach their ends.
Inputs may be any that keep to these rules, and one draw needn't show every extreme that they name: `seq_lengths`: row r holds the lengths of the two sequences packed first into device r's 256 slots; the two sum to 128 or more and to 256 at most, and in every draw some device's two sum to exactly 256.
All inputs are finite; a program needn't handle non-finite values.
Results may differ from the reference program's by a relative error of at most 0.02.
Values may be sent and summed in bfloat16 or wider, within the bound.
No kernel may reach another device: no remote copies, remote signals or barrier semaphores. Data moves between devices by JAX's collectives and lax.ppermute only.
A program may use at most 128 MiB of HBM per device.

```python
import jax
import jax.numpy as jnp
from jax import lax

D = 768
HEAD = 64
FF = 1152
TOK_DEV = 256
TOKENS = 8192
N_REPLICA = 4
N_FSDP = 8


def draw_seq_lengths(key, part):
    key = jax.random.fold_in(key, 11)
    key_total, key_full, key_first = jax.random.split(key, 3)
    row_count = N_REPLICA * N_FSDP
    totals = jax.random.randint(key_total, (row_count,), TOK_DEV // 2, TOK_DEV + 1)
    full_row = jax.random.randint(key_full, (), 0, row_count)
    row_index = jnp.arange(row_count)
    totals = jnp.where(row_index == full_row, TOK_DEV, totals)
    first_length = jax.random.randint(key_first, (row_count,), 1, totals)
    first_length = jnp.where(row_index == full_row, TOK_DEV - 1, first_length)
    second_length = totals - first_length
    return jnp.stack([first_length, second_length], 1).astype(jnp.int32)


def shard_levels(key, dims, cuts, low, largest):
    factor_of = 1.0
    for axis_at, shards_of in cuts:
        draws = jax.random.uniform(jax.random.fold_in(jax.random.fold_in(key, 6), axis_at), (shards_of,), jnp.float32, low / len(cuts), largest / len(cuts))
        factor_of = factor_of * jnp.repeat(jnp.exp(draws), dims[axis_at] // shards_of).reshape((-1,) + (1,) * (len(dims) - 1 - axis_at))
    return factor_of


def bell_draw(own_key, dims, deviation, reach, cuts=(), held_as=jnp.bfloat16):
    values = jax.random.normal(own_key, dims, jnp.float32) * deviation
    if len(cuts) > 0:
        values = shard_levels(own_key, dims, cuts, -0.22, 0.18) * values
    return jnp.clip(values, min=-reach, max=reach).astype(held_as)


def setup_inputs(seed: int = 0) -> dict:
    splits = jax.random.split(jax.random.key(seed), 10)
    tokens = bell_draw(splits[0], (TOKENS, D), 1.0, 6.0, ((0, 32),))
    seq_lengths = draw_seq_lengths(jax.random.fold_in(splits[9], 71), 0)
    norm1_gain = jnp.clip(1.0 + 0.1 * jax.random.normal(splits[2], (D,), jnp.float32), 0.5, 1.5).astype(jnp.bfloat16)
    qkv_weight = bell_draw(splits[3], (D, 3 * D), D ** -0.5, 0.21875, ((0, 8),))
    out_weight = bell_draw(splits[4], (D, D), (D // 16) ** -0.5, 0.875, ((0, 8),))
    norm2_gain = jnp.clip(1.0 + 0.1 * jax.random.normal(splits[5], (D,), jnp.float32), 0.5, 1.5).astype(jnp.bfloat16)
    in_weight = bell_draw(splits[6], (D, 2 * FF), D ** -0.5, 0.21875, ((0, 8),))
    down_weight = bell_draw(splits[7], (FF, D), FF ** -0.5, 0.1875, ((1, 8),))
    cotangent = bell_draw(splits[8], (TOKENS, D), 1.0, 6.0, ((0, 32),), jnp.float32)
    return dict(tokens=tokens, seq_lengths=seq_lengths, norm1_gain=norm1_gain, qkv_weight=qkv_weight, out_weight=out_weight, norm2_gain=norm2_gain, in_weight=in_weight, down_weight=down_weight, cotangent=cotangent)


NORM_EPS = 1e-05
ROPE_BASE = 160000.0
MASK_FILL = -1000000000.0
HIGHEST_PRECISION = lax.Precision.HIGHEST

@jax.custom_vjp
def low(v):
    return lax.optimization_barrier(v.astype(jnp.bfloat16)).astype(jnp.float32)

@jax.custom_vjp
def low_back(v):
    return v

def low_keep(v):
    return (low(v), None)

def low_pass(kept, grad):
    return (grad,)

def back_keep(v):
    return (v, None)

def back_low(kept, grad):
    return (low(grad),)
low.defvjp(low_keep, low_pass)
low_back.defvjp(back_keep, back_low)

def slot_layout(length_pairs, slot_count):
    slot_index = jnp.arange(slot_count, dtype=jnp.int32)[None, :]
    first_length = length_pairs[:, 0:1]
    both_lengths = first_length + length_pairs[:, 1:2]
    segment = jnp.where(slot_index < first_length, 0, jnp.where(slot_index < both_lengths, 1, 2)).astype(jnp.int32)
    begin = jnp.where(segment == 0, 0, jnp.where(segment == 1, first_length, both_lengths)).astype(jnp.int32)
    return (segment, (slot_index - begin).astype(jnp.int32))

def rope_tables(positions, head_size):
    half_size = head_size // 2
    frequency = ROPE_BASE ** (-(jnp.arange(half_size, dtype=jnp.float32) * 2.0) / head_size)
    angles = positions.astype(jnp.float32)[:, None] * frequency[None, :]
    return (jnp.cos(angles), jnp.sin(angles))

def rotate(values, cosine_table, sine_table):
    half_size = values.shape[-1] // 2
    first_half = values[..., :half_size]
    second_half = values[..., half_size:]
    cos_rows = cosine_table[:, None, :]
    sin_rows = sine_table[:, None, :]
    return jnp.concatenate([first_half * cos_rows - second_half * sin_rows, second_half * cos_rows + first_half * sin_rows], -1)

def norm_apply(values, gain_vector):
    row_mean = lax.optimization_barrier(jnp.mean(values, -1, keepdims=True))
    centred = values - row_mean
    row_var = lax.optimization_barrier(jnp.mean(centred * centred, -1, keepdims=True))
    return centred * lax.rsqrt(row_var + NORM_EPS) * gain_vector

def gated_unit(hidden):
    width_ff = hidden.shape[1] // 2
    return jax.nn.gelu(hidden[:, :width_ff], approximate=False) * hidden[:, width_ff:]

def forward_group(inputs, gain_one, w_qkv, w_out, gain_two, w_in, w_down, segment, positions):
    device_count, slot_count = segment.shape
    model_width = inputs.shape[1]
    head_count = model_width // HEAD
    normed = low(norm_apply(inputs, gain_one))
    joined_proj = low_back(jnp.dot(normed, w_qkv, precision=HIGHEST_PRECISION))
    cosine_table, sine_table = rope_tables(positions, HEAD)
    shape_heads = (inputs.shape[0], head_count, HEAD)
    queries = low(rotate(joined_proj[:, :model_width].reshape(shape_heads), cosine_table, sine_table))
    keys_rot = low(rotate(joined_proj[:, model_width:2 * model_width].reshape(shape_heads), cosine_table, sine_table))
    values = low(joined_proj[:, 2 * model_width:].reshape(shape_heads))
    block_shape = (device_count, slot_count, head_count, HEAD)
    scores = jnp.einsum('rthd,rshd->rhts', queries.reshape(block_shape), keys_rot.reshape(block_shape), precision=HIGHEST_PRECISION) * HEAD ** (-0.5)
    allowed = segment[:, None, :, None] == segment[:, None, None, :]
    scores = low_back(jnp.where(allowed, scores, MASK_FILL))
    probs_low = low(jax.nn.softmax(scores, axis=-1))
    context = jnp.einsum('rhts,rshd->rthd', probs_low, values.reshape(block_shape), precision=HIGHEST_PRECISION)
    context = low(low_back(context.reshape(inputs.shape[0], model_width)))
    middle = inputs + low_back(jnp.dot(context, w_out, precision=HIGHEST_PRECISION))
    normed_two = low(norm_apply(middle, gain_two))
    hidden = low_back(jnp.dot(normed_two, w_in, precision=HIGHEST_PRECISION))
    mixed = low(gated_unit(hidden))
    return middle + low_back(jnp.dot(mixed, w_down, precision=HIGHEST_PRECISION))

def reference(tokens, seq_lengths, norm1_gain, qkv_weight, out_weight, norm2_gain, in_weight, down_weight, cotangent):
    weights = (norm1_gain.astype(jnp.float32), qkv_weight.astype(jnp.float32), out_weight.astype(jnp.float32), norm2_gain.astype(jnp.float32), in_weight.astype(jnp.float32), down_weight.astype(jnp.float32))
    group_rows = N_FSDP * TOK_DEV
    inputs = tokens.astype(jnp.float32).reshape(N_REPLICA, group_rows, D)
    cotangents = cotangent.astype(jnp.float32).reshape(N_REPLICA, group_rows, D)
    length_groups = seq_lengths.reshape(N_REPLICA, N_FSDP, 2)

    def group_step(totals, group_item):
        group_inputs, group_cotangent, group_lengths = group_item
        segment, positions = slot_layout(group_lengths, TOK_DEV)
        positions = positions.reshape(group_rows)

        def apply_layer(layer_inputs, gain_one, w_qkv, w_out, gain_two, w_in, w_down):
            return forward_group(layer_inputs, gain_one, w_qkv, w_out, gain_two, w_in, w_down, segment, positions)
        result, pullback = jax.vjp(apply_layer, group_inputs, *weights)
        gradients = pullback(group_cotangent)
        summed = tuple((running + part_grad for running, part_grad in zip(totals, gradients[1:])))
        return (summed, (result.astype(jnp.bfloat16), gradients[0]))
    initial = tuple((jnp.zeros(weight.shape, jnp.float32) for weight in weights))
    totals, (outputs, grad_inputs) = lax.scan(group_step, initial, (inputs, cotangents, length_groups))
    return (outputs.reshape(TOKENS, D), grad_inputs.reshape(TOKENS, D), totals[0], totals[1], totals[2], totals[3], totals[4], totals[5])
```

```python
import jax
import jax.numpy as jnp
from jax import lax
from jax.experimental import pallas as pl
from jax.experimental.pallas import tpu as pltpu
from jax.sharding import PartitionSpec as P

HEAD = 64


NORM_EPS = 1e-05
ROPE_BASE = 160000.0
MASK_FILL = -1000000000.0


def slot_layout(length_pairs, slot_count):
    slot_index = jnp.arange(slot_count, dtype=jnp.int32)[None, :]
    first_length = length_pairs[:, 0:1]
    both_lengths = first_length + length_pairs[:, 1:2]
    segment = jnp.where(
        slot_index < first_length, 0, jnp.where(slot_index < both_lengths, 1, 2)
    ).astype(jnp.int32)
    begin = jnp.where(segment == 0, 0, jnp.where(segment == 1, first_length, both_lengths))
    return (segment, slot_index - begin)


def rope_tables(positions, head_size):
    half_size = head_size // 2
    frequency = ROPE_BASE ** (-(jnp.arange(half_size, dtype=jnp.float32) * 2.0) / head_size)
    angles = positions.astype(jnp.float32)[:, None] * frequency[None, :]
    return (jnp.cos(angles), jnp.sin(angles))


def rotate(values, cosine_table, sine_table):
    half_size = values.shape[-1] // 2
    first_half = values[..., :half_size]
    second_half = values[..., half_size:]
    cos_rows = cosine_table[:, None, :]
    sin_rows = sine_table[:, None, :]
    return jnp.concatenate(
        [
            first_half * cos_rows - second_half * sin_rows,
            second_half * cos_rows + first_half * sin_rows,
        ],
        -1,
    )


def norm_apply(values, gain_vector):
    row_mean = jnp.mean(values, -1, keepdims=True)
    centred = values - row_mean
    row_var = jnp.mean(centred * centred, -1, keepdims=True)
    return centred * lax.rsqrt(row_var + NORM_EPS) * gain_vector


def gated_unit(hidden):
    width_ff = hidden.shape[1] // 2
    return jax.nn.gelu(hidden[:, :width_ff], approximate=False) * hidden[:, width_ff:]


CORE, ALONG_X, ALONG_Y = 1, 2, 4
F32, BF16 = jnp.float32, jnp.bfloat16


def swap(values, mask):
    return lax.ppermute(values, "fsdp", [(i, i ^ mask) for i in range(8)])


def gather_pieces(own):
    half = own.shape[0] // 2
    from_x = swap(own, ALONG_X)
    from_y = swap(own, ALONG_Y)
    diag_a = swap(from_y[:half], ALONG_X)
    diag_b = swap(from_x[half:], ALONG_Y)
    mine = [own, from_x, from_y, diag_a, diag_b]
    return mine + [swap(piece, CORE) for piece in mine]


PIECE_PLACES = [
    (mask | core, first)
    for core in (0, CORE)
    for mask, first in ((0, 0), (ALONG_X, 0), (ALONG_Y, 0), (6, 0), (6, 1))
]


def assemble(pieces, widths):
    own_rows = pieces[0].shape[0]
    row_count = 8 * own_rows

    def kernel(*refs):
        sources, targets, semaphores = refs[:10], refs[10:-1], refs[-1]
        me = lax.axis_index("fsdp")
        copies = []
        for at, (mask, first) in enumerate(PIECE_PLACES):
            rows = pieces[at].shape[0]
            start = pl.multiple_of((me ^ mask) * own_rows + first * (own_rows // 2), own_rows // 2)
            lane = 0
            for to, width in enumerate(widths):
                copies.append(
                    pltpu.make_async_copy(
                        sources[at].at[:, pl.ds(lane, width)],
                        targets[to].at[pl.ds(start, rows), :],
                        semaphores.at[at, to],
                    )
                )
                lane += width
        for copy in copies:
            copy.start()
        for copy in copies:
            copy.wait()

    return pl.pallas_call(
        kernel,
        out_shape=[jax.ShapeDtypeStruct((row_count, width), BF16) for width in widths],
        in_specs=[pl.BlockSpec(memory_space=pl.ANY)] * 10,
        out_specs=[pl.BlockSpec(memory_space=pl.ANY)] * len(widths),
        scratch_shapes=[pltpu.SemaphoreType.DMA((10, len(widths)))],
        name="assemble",
    )(*pieces)


LEAVING = [(6, 0), (ALONG_X, 0), (6, 1), (ALONG_Y, 1), (ALONG_X, 1), (ALONG_Y, 0), (0, 0), (0, 1)]


def weight_grad(rows_side, columns_side):
    slots, model_width = rows_side.shape
    width = columns_side.shape[1]
    half = model_width // 16
    step = 384

    def kernel(rows_ref, columns_ref, keep_ref, send_ref, turned, picked):
        me = lax.axis_index("fsdp")
        turned[...] = rows_ref[...].astype(F32).T.astype(BF16)
        for core in (0, CORE):
            for at, (mask, first) in enumerate(LEAVING):
                start = pl.multiple_of((me ^ (mask | core)) * (2 * half) + first * half, half)
                picked[pl.ds((core * 8 + at) * half, half), :] = turned[pl.ds(start, half), :]
        for lane in range(0, width, step):
            product = jnp.dot(
                picked[...], columns_ref[:, lane : lane + step], preferred_element_type=F32
            ).astype(BF16)
            keep_ref[:, lane : lane + step] = product[: 8 * half]
            send_ref[:, lane : lane + step] = product[8 * half :]

    vmem = pl.BlockSpec(memory_space=pltpu.VMEM)
    shape = jax.ShapeDtypeStruct((8 * half, width), BF16)
    return pl.pallas_call(
        kernel,
        out_shape=[shape, shape],
        in_specs=[vmem, vmem],
        out_specs=[vmem, vmem],
        scratch_shapes=[
            pltpu.VMEM((model_width, slots), BF16),
            pltpu.VMEM((model_width, slots), BF16),
        ],
        compiler_params=pltpu.CompilerParams(vmem_limit_bytes=40 * 2**20),
        cost_estimate=pl.CostEstimate(
            flops=2 * slots * model_width * width,
            bytes_accessed=2 * (slots * (model_width + width) + model_width * width),
            transcendentals=0,
        ),
        name="weight_grad",
    )(rows_side, columns_side)


def gather_rows(own, widths):
    if lax.axis_size("fsdp") == 8:
        return assemble(gather_pieces(own), widths)
    whole = lax.all_gather(own, "fsdp", axis=0, tiled=True)
    edges = [sum(widths[:at]) for at in range(1, len(widths))]
    return jnp.split(whole, edges, 1)


def shard_grad(rows_side, columns_side):
    if lax.axis_size("fsdp") == 8:
        return scatter_sum(*weight_grad(rows_side, columns_side))
    whole = jnp.einsum("tc,tf->cf", rows_side, columns_side, preferred_element_type=F32)
    shard = lax.psum_scatter(whole.astype(BF16), "fsdp", scatter_dimension=0, tiled=True)
    return shard.astype(F32)


def add(*parts):
    return sum(part.astype(F32) for part in parts).astype(BF16)


def scatter_sum(keep, send):
    half = keep.shape[0] // 8
    other = swap(send, CORE)

    def chip(first, count):
        rows = slice(first * half, (first + count) * half)
        return add(keep[rows], other[rows])

    by_x = swap(chip(0, 2), ALONG_X)
    by_y = swap(chip(2, 2), ALONG_Y)
    late_x = swap(add(keep[4 * half : 5 * half], other[4 * half : 5 * half], by_y[:half]), ALONG_X)
    late_y = swap(add(keep[5 * half : 6 * half], other[5 * half : 6 * half], by_x[:half]), ALONG_Y)
    own = keep[6 * half :].astype(F32) + other[6 * half :].astype(F32)
    own += jnp.concatenate([by_x[half:], by_y[half:]], 0).astype(F32)
    own += jnp.concatenate([late_y, late_x], 0).astype(F32)
    return own


def copies_sum(values):
    copies = lax.axis_size("replica")
    me = lax.axis_index("replica")
    rows, width = values.shape
    part = rows // copies
    narrow = values.astype(BF16)

    def shift(array, by):
        return lax.ppermute(array, "replica", [(i, (i + by) % copies) for i in range(copies)])

    def part_of(array, at):
        return lax.dynamic_slice_in_dim(array, at * part, part, 0)

    total = part_of(values, me)
    for by in range(1, copies):
        total += shift(part_of(narrow, (me + by) % copies), by).astype(F32)
    total = total.astype(BF16)
    result = jnp.zeros((copies, part, width), BF16)
    result = lax.dynamic_update_index_in_dim(result, total, me, 0)
    for by in range(1, copies):
        result = lax.dynamic_update_index_in_dim(
            result, shift(total, by), (me + copies - by) % copies, 0
        )
    return result.reshape(rows, width).astype(F32)


def per_device(
    tokens,
    seq_lengths,
    norm1_gain,
    qkv_weight,
    out_weight,
    norm2_gain,
    in_weight,
    down_weight,
    cotangent,
):
    wide = qkv_weight.shape[1]
    out_width = out_weight.shape[1]
    ff_width = down_weight.shape[0]
    gain_columns = jnp.pad(
        jnp.stack([norm1_gain, norm2_gain], 1), ((0, 0), (0, 126))
    )
    w_qkv, w_out, gains = gather_rows(
        jnp.concatenate([qkv_weight, out_weight, gain_columns], 1), (wide, out_width, 128)
    )
    w_in, w_down_t = gather_rows(
        jnp.concatenate([in_weight, down_weight.T], 1), (wide, ff_width)
    )
    gain_one = gains[:, 0].astype(F32)
    gain_two = gains[:, 1].astype(F32)
    slot_count, model_width = tokens.shape
    head_count = model_width // HEAD
    segment, positions = slot_layout(seq_lengths, slot_count)
    segment = segment[0]
    positions = positions[0]
    cosine_table, sine_table = rope_tables(positions, HEAD)
    allowed = (segment[:, None] == segment[None, :])[None]
    score_scale = HEAD ** (-0.5)
    inputs = tokens.astype(jnp.float32)
    normed, norm_one_pull = jax.vjp(norm_apply, inputs, gain_one)
    normed_b = normed.astype(jnp.bfloat16)
    joined_proj = jnp.dot(normed_b, w_qkv, preferred_element_type=jnp.float32)
    shape_heads = (slot_count, head_count, HEAD)

    def rope_pair(raw_queries, raw_keys):
        return (
            rotate(raw_queries, cosine_table, sine_table),
            rotate(raw_keys, cosine_table, sine_table),
        )

    rotated, rope_pull = jax.vjp(
        rope_pair,
        joined_proj[:, :model_width].reshape(shape_heads),
        joined_proj[:, model_width : 2 * model_width].reshape(shape_heads),
    )
    queries_b = rotated[0].astype(jnp.bfloat16)
    keys_b = rotated[1].astype(jnp.bfloat16)
    values_b = joined_proj[:, 2 * model_width :].reshape(shape_heads).astype(jnp.bfloat16)

    def masked_scores():
        raw_scores = (
            jnp.einsum("thd,shd->hts", queries_b, keys_b, preferred_element_type=jnp.float32)
            * score_scale
        )
        return jnp.where(allowed, raw_scores, MASK_FILL)

    scores = masked_scores()
    row_top = jnp.max(scores, -1, keepdims=True)
    exponent = jnp.exp(scores - row_top)
    row_total = jnp.sum(exponent, -1, keepdims=True)
    probs_b = (exponent / row_total).astype(jnp.bfloat16)
    context_b = jnp.einsum("hts,shd->thd", probs_b, values_b, preferred_element_type=jnp.float32)
    context_b = context_b.reshape(slot_count, model_width).astype(jnp.bfloat16)
    middle = inputs + jnp.dot(context_b, w_out, preferred_element_type=jnp.float32)
    normed_two, norm_two_pull = jax.vjp(norm_apply, middle, gain_two)
    normed_two_b = normed_two.astype(jnp.bfloat16)
    hidden = jnp.dot(normed_two_b, w_in, preferred_element_type=jnp.float32)
    activated, gate_pull = jax.vjp(gated_unit, hidden)
    mixed_b = activated.astype(jnp.bfloat16)
    output = (middle + jnp.einsum("tf,df->td", mixed_b, w_down_t, preferred_element_type=jnp.float32)).astype(
        jnp.bfloat16
    )
    grad_out_b = cotangent.astype(jnp.bfloat16)
    down_shard = shard_grad(grad_out_b, mixed_b)
    grad_mixed = jnp.einsum("td,df->tf", grad_out_b, w_down_t, preferred_element_type=jnp.float32)
    grad_hidden_b = gate_pull(grad_mixed)[0].astype(jnp.bfloat16)
    in_shard = shard_grad(normed_two_b, grad_hidden_b)
    grad_normed_two = jnp.einsum(
        "tf,cf->tc", grad_hidden_b, w_in, preferred_element_type=jnp.float32
    )
    grad_mid_norm = norm_two_pull(grad_normed_two)[0]
    grad_middle = cotangent + grad_mid_norm
    grad_middle_b = grad_middle.astype(jnp.bfloat16)
    out_shard = shard_grad(context_b, grad_middle_b)
    grad_context = jnp.einsum("td,cd->tc", grad_middle_b, w_out, preferred_element_type=jnp.float32)
    grad_context_b = grad_context.reshape(shape_heads).astype(jnp.bfloat16)
    probs_again = jnp.exp(masked_scores() - row_top) / row_total
    probs_again_b = probs_again.astype(jnp.bfloat16)
    grad_probs = jnp.einsum(
        "thd,shd->hts", grad_context_b, values_b, preferred_element_type=jnp.float32
    )
    grad_values = jnp.einsum(
        "hts,thd->shd", probs_again_b, grad_context_b, preferred_element_type=jnp.float32
    )
    row_inner = jnp.sum(probs_again * grad_probs, -1, keepdims=True)
    grad_scores_b = (probs_again * (grad_probs - row_inner)).astype(jnp.bfloat16)
    grad_queries = (
        jnp.einsum("hts,shd->thd", grad_scores_b, keys_b, preferred_element_type=jnp.float32)
        * score_scale
    )
    grad_keys = (
        jnp.einsum("hts,thd->shd", grad_scores_b, queries_b, preferred_element_type=jnp.float32)
        * score_scale
    )
    raw_grads = rope_pull((grad_queries, grad_keys))
    grad_joined_b = jnp.concatenate(
        [
            raw_grads[0].reshape(slot_count, model_width),
            raw_grads[1].reshape(slot_count, model_width),
            grad_values.reshape(slot_count, model_width),
        ],
        1,
    ).astype(jnp.bfloat16)
    qkv_shard = shard_grad(normed_b, grad_joined_b)
    grad_normed = jnp.einsum("tf,cf->tc", grad_joined_b, w_qkv, preferred_element_type=jnp.float32)
    grad_in_norm = norm_one_pull(grad_normed)[0]
    grad_tokens = grad_middle + grad_in_norm
    mlp_sum = copies_sum(jnp.concatenate([in_shard, down_shard], 1))
    attn_sum = copies_sum(jnp.concatenate([qkv_shard, out_shard], 1))
    grad_qkv, grad_w_out = attn_sum[:, :wide], attn_sum[:, wide:]
    grad_in, grad_down = mlp_sum[:, :wide], mlp_sum[:, wide:].T

    def gain_grad(weight, weight_sum, gain):
        return jnp.sum(weight.astype(F32) * weight_sum, 1) / gain.astype(F32)

    return (
        output,
        grad_tokens,
        gain_grad(qkv_weight, grad_qkv, norm1_gain),
        grad_qkv,
        grad_w_out,
        gain_grad(in_weight, grad_in, norm2_gain),
        grad_in,
        grad_down,
    )


def solution(mesh):
    return jax.shard_map(
        per_device,
        mesh=mesh,
        in_specs=(
            P(("replica", "fsdp"), None),
            P(("replica", "fsdp"), None),
            P("fsdp"),
            P("fsdp", None),
            P("fsdp", None),
            P("fsdp"),
            P("fsdp", None),
            P(None, "fsdp"),
            P(("replica", "fsdp"), None),
        ),
        out_specs=(
            P(("replica", "fsdp"), None),
            P(("replica", "fsdp"), None),
            P("fsdp"),
            P("fsdp", None),
            P("fsdp", None),
            P("fsdp"),
            P("fsdp", None),
            P(None, "fsdp"),
        ),
        check_vma=False,
    )
```

```python
import jax
import jax.numpy as jnp
from jax import lax
from jax.experimental import pallas as pl
from jax.experimental.pallas import tpu as pltpu
from jax.sharding import PartitionSpec as P

HEAD = 64


NORM_EPS = 1e-05
ROPE_BASE = 160000.0
MASK_FILL = -1000000000.0


def slot_layout(length_pairs, slot_count):
    slot_index = jnp.arange(slot_count, dtype=jnp.int32)[None, :]
    first_length = length_pairs[:, 0:1]
    both_lengths = first_length + length_pairs[:, 1:2]
    segment = jnp.where(
        slot_index < first_length, 0, jnp.where(slot_index < both_lengths, 1, 2)
    ).astype(jnp.int32)
    begin = jnp.where(segment == 0, 0, jnp.where(segment == 1, first_length, both_lengths))
    return (segment, slot_index - begin)


def rope_tables(positions, head_size):
    half_size = head_size // 2
    frequency = ROPE_BASE ** (-(jnp.arange(half_size, dtype=jnp.float32) * 2.0) / head_size)
    angles = positions.astype(jnp.float32)[:, None] * frequency[None, :]
    return (jnp.cos(angles), jnp.sin(angles))


CORE, ALONG_X, ALONG_Y = 1, 2, 4
F32, BF16 = jnp.float32, jnp.bfloat16
VMEM = pl.BlockSpec(memory_space=pltpu.VMEM)
LANES = 128
STEP = 384


def run_kernel(body, name, outs, scratch, operands, scalars=0, flops=0):
    smem = pl.BlockSpec(memory_space=pltpu.SMEM)
    return pl.pallas_call(
        body,
        out_shape=[jax.ShapeDtypeStruct(shape, kind) for shape, kind in outs],
        in_specs=[smem] * scalars + [VMEM] * (len(operands) - scalars),
        out_specs=[VMEM] * len(outs),
        scratch_shapes=scratch,
        compiler_params=pltpu.CompilerParams(vmem_limit_bytes=48 * 2**20),
        cost_estimate=pl.CostEstimate(flops=flops, bytes_accessed=0, transcendentals=0),
        name=name,
    )(*operands)


def swap(values, mask):
    return lax.ppermute(values, "fsdp", [(i, i ^ mask) for i in range(8)])


def gather_pieces(own):
    half = own.shape[0] // 2
    from_x = swap(own, ALONG_X)
    from_y = swap(own, ALONG_Y)
    diag_a = swap(from_y[:half], ALONG_X)
    diag_b = swap(from_x[half:], ALONG_Y)
    mine = [own, from_x, from_y, diag_a, diag_b]
    return mine + [swap(piece, CORE) for piece in mine]


PIECE_PLACES = [
    (mask | core, first)
    for core in (0, CORE)
    for mask, first in ((0, 0), (ALONG_X, 0), (ALONG_Y, 0), (6, 0), (6, 1))
]


def gathered(own):
    if lax.axis_size("fsdp") == 8:
        return gather_pieces(own)
    return [lax.all_gather(own, "fsdp", axis=0, tiled=True)]


def lay_out(pieces, targets):
    if len(pieces) == 1:
        places = [(0, 0)]
        me, own_rows = 0, pieces[0].shape[0]
    else:
        places = PIECE_PLACES
        me, own_rows = lax.axis_index("fsdp"), pieces[0].shape[0]
    for piece, (mask, first) in zip(pieces, places):
        rows = piece.shape[0]
        start = (me ^ mask) * own_rows + first * (own_rows // 2)
        start = 0 if len(pieces) == 1 else pl.multiple_of(start, own_rows // 2)
        lane = 0
        for target in targets:
            width = target.shape[1]
            target[pl.ds(start, rows), :] = piece[:, lane : lane + width]
            lane += width


LEAVING = [(6, 0), (ALONG_X, 0), (6, 1), (ALONG_Y, 1), (ALONG_X, 1), (ALONG_Y, 0), (0, 0), (0, 1)]


def pick_rows(values, turned, picked):
    if picked is None:
        turned[...] = values.astype(F32).T.astype(BF16)
        return
    half = turned.shape[0] // 16
    me = lax.axis_index("fsdp")
    turned[...] = values.astype(F32).T.astype(BF16)
    for core in (0, CORE):
        for at, (mask, first) in enumerate(LEAVING):
            start = pl.multiple_of((me ^ (mask | core)) * (2 * half) + first * half, half)
            picked[pl.ds((core * 8 + at) * half, half), :] = turned[pl.ds(start, half), :]


def write_grad(lhs, columns, outs):
    width = columns.shape[1]
    for lane in range(0, width, STEP):
        product = jnp.dot(
            lhs[...], columns[:, lane : lane + STEP], preferred_element_type=F32
        ).astype(BF16)
        row = 0
        for out in outs:
            out[:, lane : lane + STEP] = product[row : row + out.shape[0]]
            row += out.shape[0]


def grad_outs(model_width, width):
    if lax.axis_size("fsdp") == 8:
        return [((model_width // 2, width), BF16)] * 2
    return [((model_width, width), BF16)]


def grad_scratch(model_width, slots):
    one = pltpu.VMEM((model_width, slots), BF16)
    return [one, one] if lax.axis_size("fsdp") == 8 else [one]


def write_weight_grad(rows_side, columns, outs, scratch):
    pick_rows(rows_side, scratch[0], scratch[1] if len(scratch) > 1 else None)
    write_grad(scratch[-1], columns, outs)


def dot_nt(a, b):
    return lax.dot_general(a, b, (((1,), (1,)), ((), ())), preferred_element_type=F32)


def dot_tn(a, b):
    return lax.dot_general(a, b, (((0,), (0,)), ((), ())), preferred_element_type=F32)


def dot_nn(a, b):
    return jnp.dot(a, b, preferred_element_type=F32)


def normalised(values):
    mean = jnp.mean(values, -1, keepdims=True)
    centred = values - mean
    scale = lax.rsqrt(jnp.mean(centred * centred, -1, keepdims=True) + NORM_EPS)
    return centred * scale, scale


def norm_back(grad, xhat, scale, gain):
    scaled = grad * gain
    mean = jnp.mean(scaled, -1, keepdims=True)
    along = jnp.mean(scaled * xhat, -1, keepdims=True)
    return scale * (scaled - mean - xhat * along)


def turn_halves(block, cosine, sine):
    lane = lax.broadcasted_iota(jnp.int32, block.shape, 1)
    low_half = (lane % HEAD) < HEAD // 2
    other = jnp.where(
        low_half,
        pltpu.roll(block, LANES - HEAD // 2, 1),
        pltpu.roll(block, HEAD // 2, 1),
    )
    return block * cosine + other * sine


def head_lanes(shape, head):
    lane = lax.broadcasted_iota(jnp.int32, shape, 1)
    return (lane // HEAD) == head


def only(values, head):
    return jnp.where(head_lanes(values.shape, head), values, jnp.zeros_like(values))


def attention_forward(lengths, tokens, cosine, sine, pieces, qkv_width, out_width):
    slots, model_width = tokens.shape
    count = len(pieces)

    def body(*refs):
        lengths_ref, tokens_ref, cosine_ref, sine_ref = refs[:4]
        piece_refs = refs[4 : 4 + count]
        (h1_ref, q_ref, k_ref, v_ref, probs_ref, context_ref, middle_ref, h2_ref, w_qkv, w_out,
         gain_rows, gain_columns, joined) = refs[4 + count :]
        lay_out(piece_refs, [w_qkv, w_out, gain_columns])
        gain_rows[...] = gain_columns[...].astype(F32).T[:8]
        inputs = tokens_ref[...].astype(F32)
        h1_ref[...] = (normalised(inputs)[0] * gain_rows[0:1, :]).astype(BF16)
        for lane in range(0, qkv_width, model_width):
            joined[:, lane : lane + model_width] = dot_nn(
                h1_ref[...], w_qkv[:, lane : lane + model_width]
            )
        first = lengths_ref[0, 0]
        both = first + lengths_ref[0, 1]

        def segment(axis):
            slot = lax.broadcasted_iota(jnp.int32, (slots, slots), axis)
            return (slot >= first).astype(jnp.int32) + (slot >= both).astype(jnp.int32)

        allowed = segment(0) == segment(1)
        cosine_rows, sine_rows = cosine_ref[...], sine_ref[...]
        for lane in range(0, model_width, LANES):
            block = slice(lane, lane + LANES)

            def rope(offset):
                raw = joined[:, offset + lane : offset + lane + LANES]
                return turn_halves(raw, cosine_rows, sine_rows)

            query = (rope(0) * HEAD ** (-0.5)).astype(BF16)
            key = rope(model_width).astype(BF16)
            value = joined[:, 2 * model_width + lane : 2 * model_width + lane + LANES].astype(BF16)
            q_ref[:, block] = query
            k_ref[:, block] = key
            v_ref[:, block] = value
            context = None
            for head in range(2):
                scores = jnp.where(allowed, dot_nt(only(query, head), key), MASK_FILL)
                exponent = jnp.exp(scores - jnp.max(scores, -1, keepdims=True))
                total = jnp.sum(exponent, -1, keepdims=True)
                probs = (exponent * (1.0 / total)).astype(BF16)
                probs_ref[lane // HEAD + head] = probs
                part = dot_nn(probs, only(value, head))
                context = part if context is None else context + part
            context_ref[:, block] = context.astype(BF16)
        middle = inputs + dot_nn(context_ref[...], w_out[...])
        middle_ref[...] = middle
        h2_ref[...] = (normalised(middle)[0] * gain_rows[1:2, :]).astype(BF16)

    wide = (slots, model_width)
    return run_kernel(
        body,
        "attention_forward",
        [(wide, BF16)] * 4
        + [((model_width // HEAD, slots, slots), BF16), (wide, BF16), (wide, F32), (wide, BF16)]
        + [((model_width, qkv_width), BF16), ((model_width, out_width), BF16)]
        + [((8, model_width), F32)],
        [pltpu.VMEM((model_width, LANES), BF16), pltpu.VMEM((slots, qkv_width), F32)],
        [lengths, tokens, cosine, sine, *pieces],
        scalars=1,
    )


ERF_UP = (0.00022905065861350646, 0.0034082910107109506, 0.050955695062380861,
          0.18520832239976145, 1.128379143519084)
ERF_DOWN = (-1.1791602954361697e-7, 0.000023547966471313185, 0.0010179625278914885,
            0.014070470171167667, 0.11098505178285362, 0.49746925110067538, 1.0)


def erf(values):
    values = jnp.clip(values, -3.832506856900711, 3.832506856900711)
    square = values * values
    up = jnp.full_like(values, ERF_UP[0])
    for term in ERF_UP[1:]:
        up = up * square + term
    down = jnp.full_like(values, ERF_DOWN[0])
    for term in ERF_DOWN[1:]:
        down = down * square + term
    return values * up / down


def feed_forward(h2, cotangent, pieces, in_width, ff_width):
    slots, model_width = h2.shape
    count = len(pieces)
    outs = grad_outs(model_width, ff_width)
    scratch = grad_scratch(model_width, slots)

    def body(*refs):
        h2_ref, cotangent_ref = refs[:2]
        piece_refs = refs[2 : 2 + count]
        mixed_ref, grad_hidden_ref, w_in, w_down_t = refs[2 + count : 6 + count]
        grad_refs = refs[6 + count : 6 + count + len(outs)]
        turning = refs[6 + count + len(outs) :]
        lay_out(piece_refs, [w_in, w_down_t])
        grad_out = cotangent_ref[...].astype(BF16)
        for lane in range(0, ff_width, STEP):
            here, there = slice(lane, lane + STEP), slice(ff_width + lane, ff_width + lane + STEP)
            raw = dot_nn(h2_ref[...], w_in[:, here])
            gate = dot_nn(h2_ref[...], w_in[:, there])
            grad_mixed = dot_nn(grad_out, w_down_t[:, here])
            below = 0.5 * (1.0 + erf(raw * 0.7071067811865476))
            bell = jnp.exp(raw * raw * -0.5) * 0.3989422804014327
            active = raw * below
            mixed_ref[:, here] = (active * gate).astype(BF16)
            grad_hidden_ref[:, here] = (grad_mixed * gate * (below + raw * bell)).astype(BF16)
            grad_hidden_ref[:, there] = (grad_mixed * active).astype(BF16)
        write_weight_grad(cotangent_ref[...], mixed_ref, grad_refs, turning)

    results = run_kernel(
        body,
        "feed_forward",
        [((slots, ff_width), BF16), ((slots, in_width), BF16)]
        + [((model_width, in_width), BF16), ((model_width, ff_width), BF16)]
        + outs,
        scratch,
        [h2, cotangent, *pieces],
    )
    return results[:4], results[4:]


def weight_grad(rows_side, columns_side):
    slots, model_width = rows_side.shape
    outs = grad_outs(model_width, columns_side.shape[1])

    def body(rows_ref, columns_ref, *refs):
        write_weight_grad(rows_ref[...], columns_ref, refs[: len(outs)], refs[len(outs) :])

    return run_kernel(
        body, "weight_grad", outs, grad_scratch(model_width, slots), [rows_side, columns_side]
    )


def middle_backward(grad_hidden, w_in, middle, gains, cotangent, w_out, context):
    slots, model_width = middle.shape
    outs = grad_outs(model_width, w_out.shape[1])

    def body(grad_hidden_ref, w_in_ref, middle_ref, gains_ref, cotangent_ref, w_out_ref,
             context_ref, grad_middle_ref, grad_context_ref, *refs):
        grad_h2 = dot_nt(grad_hidden_ref[...], w_in_ref[...])
        xhat, scale = normalised(middle_ref[...])
        grad_middle = cotangent_ref[...] + norm_back(grad_h2, xhat, scale, gains_ref[1:2, :])
        grad_middle_ref[...] = grad_middle
        narrow = grad_middle.astype(BF16)
        grad_context_ref[...] = dot_nt(narrow, w_out_ref[...]).astype(BF16)
        write_weight_grad(
            context_ref[...], narrow, refs[: len(outs)], refs[len(outs) :]
        )

    wide = (slots, model_width)
    results = run_kernel(
        body,
        "middle_backward",
        [(wide, F32), (wide, BF16)] + outs,
        grad_scratch(model_width, slots),
        [grad_hidden, w_in, middle, gains, cotangent, w_out, context],
    )
    return results[:2], results[2:]


def attention_backward(query, key, value, probs, context, grad_context, cosine, sine, h1):
    slots, model_width = query.shape
    outs = grad_outs(model_width, 3 * model_width)

    def body(q_ref, k_ref, v_ref, probs_ref, context_ref, grad_context_ref, cosine_ref, sine_ref,
             h1_ref, joined_ref, *refs):
        cosine_rows, sine_rows = cosine_ref[...], -sine_ref[...]
        for lane in range(0, model_width, LANES):
            block = slice(lane, lane + LANES)
            query, key, value = q_ref[:, block], k_ref[:, block], v_ref[:, block]
            grad = grad_context_ref[:, block]
            product = grad.astype(F32) * context_ref[:, block].astype(F32)
            grad_query = grad_key = grad_value = 0.0
            for head in range(2):
                here = probs_ref[lane // HEAD + head]
                inner = jnp.sum(only(product, head), -1, keepdims=True)
                grad_probs = dot_nt(only(grad, head), value)
                grad_scores = (here.astype(F32) * (grad_probs - inner)).astype(BF16)
                grad_value += dot_tn(only(grad, head), here)
                grad_query += dot_nn(grad_scores, only(key, head))
                grad_key += dot_tn(only(query, head), grad_scores)
            grad_query = turn_halves(grad_query * HEAD ** (-0.5), cosine_rows, sine_rows)
            grad_key = turn_halves(grad_key.T, cosine_rows, sine_rows)
            joined_ref[:, block] = grad_query.astype(BF16)
            joined_ref[:, model_width + lane : model_width + lane + LANES] = grad_key.astype(BF16)
            joined_ref[:, 2 * model_width + lane : 2 * model_width + lane + LANES] = (
                grad_value.T.astype(BF16)
            )
        write_weight_grad(h1_ref[...], joined_ref, refs[: len(outs)], refs[len(outs) :])

    results = run_kernel(
        body,
        "attention_backward",
        [((slots, 3 * model_width), BF16)] + outs,
        grad_scratch(model_width, slots),
        [query, key, value, probs, context, grad_context, cosine, sine, h1],
    )
    return results[0], results[1:]


def finish(tokens, middle, mixed, w_down_t, grad_joined, w_qkv, grad_middle, gains):
    def body(tokens_ref, middle_ref, mixed_ref, w_down_ref, joined_ref, w_qkv_ref,
             grad_middle_ref, gains_ref, output_ref, grad_ref):
        output = middle_ref[...] + dot_nt(mixed_ref[...], w_down_ref[...])
        output_ref[...] = output.astype(BF16)
        grad_h1 = dot_nt(joined_ref[...], w_qkv_ref[...])
        xhat, scale = normalised(tokens_ref[...].astype(F32))
        grad_ref[...] = grad_middle_ref[...] + norm_back(grad_h1, xhat, scale, gains_ref[0:1, :])

    return run_kernel(
        body,
        "finish",
        [(tokens.shape, BF16), (tokens.shape, F32)],
        [],
        [tokens, middle, mixed, w_down_t, grad_joined, w_qkv, grad_middle, gains],
    )


def add(*parts):
    return sum(part.astype(F32) for part in parts).astype(BF16)


def scatter_sum(parts):
    if len(parts) == 1:
        return lax.psum_scatter(parts[0], "fsdp", scatter_dimension=0, tiled=True).astype(F32)
    keep, send = parts
    half = keep.shape[0] // 8
    other = swap(send, CORE)

    def chip(first, count):
        rows = slice(first * half, (first + count) * half)
        return add(keep[rows], other[rows])

    by_x = swap(chip(0, 2), ALONG_X)
    by_y = swap(chip(2, 2), ALONG_Y)
    late_x = swap(add(keep[4 * half : 5 * half], other[4 * half : 5 * half], by_y[:half]), ALONG_X)
    late_y = swap(add(keep[5 * half : 6 * half], other[5 * half : 6 * half], by_x[:half]), ALONG_Y)
    own = keep[6 * half :].astype(F32) + other[6 * half :].astype(F32)
    own += jnp.concatenate([by_x[half:], by_y[half:]], 0).astype(F32)
    own += jnp.concatenate([late_y, late_x], 0).astype(F32)
    return own


def copies_sum(values):
    copies = lax.axis_size("replica")
    me = lax.axis_index("replica")
    rows, width = values.shape
    part = rows // copies
    narrow = values.astype(BF16)

    def shift(array, by):
        return lax.ppermute(array, "replica", [(i, (i + by) % copies) for i in range(copies)])

    def part_of(array, at):
        return lax.dynamic_slice_in_dim(array, at * part, part, 0)

    total = part_of(values, me)
    for by in range(1, copies):
        total += shift(part_of(narrow, (me + by) % copies), by).astype(F32)
    total = total.astype(BF16)
    result = jnp.zeros((copies, part, width), BF16)
    result = lax.dynamic_update_index_in_dim(result, total, me, 0)
    for by in range(1, copies):
        result = lax.dynamic_update_index_in_dim(
            result, shift(total, by), (me + copies - by) % copies, 0
        )
    return result.reshape(rows, width).astype(F32)


def per_device(
    tokens,
    seq_lengths,
    norm1_gain,
    qkv_weight,
    out_weight,
    norm2_gain,
    in_weight,
    down_weight,
    cotangent,
):
    slot_count = tokens.shape[0]
    qkv_width, out_width = qkv_weight.shape[1], out_weight.shape[1]
    in_width, ff_width = in_weight.shape[1], down_weight.shape[0]
    gain_columns = jnp.pad(jnp.stack([norm1_gain, norm2_gain], 1), ((0, 0), (0, LANES - 2)))
    attn_pieces = gathered(jnp.concatenate([qkv_weight, out_weight, gain_columns], 1))
    mlp_pieces = gathered(jnp.concatenate([in_weight, down_weight.T], 1))
    positions = slot_layout(seq_lengths, slot_count)[1][0]
    cosine, sine = rope_tables(positions, HEAD)
    cosine = jnp.concatenate([cosine] * 4, 1)
    sine = jnp.concatenate([-sine, sine, -sine, sine], 1)

    (h1, query, key, value, probs, context, middle, h2, w_qkv, w_out, gains) = attention_forward(
        seq_lengths, tokens, cosine, sine, attn_pieces, qkv_width, out_width
    )
    (mixed, grad_hidden, w_in, w_down_t), down_parts = feed_forward(
        h2, cotangent, mlp_pieces, in_width, ff_width
    )
    down_shard = scatter_sum(down_parts)
    in_shard = scatter_sum(weight_grad(h2, grad_hidden))
    (grad_middle, grad_context), out_parts = middle_backward(
        grad_hidden, w_in, middle, gains, cotangent, w_out, context
    )
    out_shard = scatter_sum(out_parts)
    grad_joined, qkv_parts = attention_backward(
        query, key, value, probs, context, grad_context, cosine, sine, h1
    )
    qkv_shard = scatter_sum(qkv_parts)
    output, grad_tokens = finish(
        tokens, middle, mixed, w_down_t, grad_joined, w_qkv, grad_middle, gains
    )
    mlp_sum = copies_sum(jnp.concatenate([in_shard, down_shard], 1))
    attn_sum = copies_sum(jnp.concatenate([qkv_shard, out_shard], 1))
    grad_qkv, grad_out = attn_sum[:, :qkv_width], attn_sum[:, qkv_width:]
    grad_in, grad_down = mlp_sum[:, :in_width], mlp_sum[:, in_width:].T

    def gain_grad(weight, weight_sum, gain):
        return jnp.sum(weight.astype(F32) * weight_sum, 1) / gain.astype(F32)

    return (
        output,
        grad_tokens,
        gain_grad(qkv_weight, grad_qkv, norm1_gain),
        grad_qkv,
        grad_out,
        gain_grad(in_weight, grad_in, norm2_gain),
        grad_in,
        grad_down,
    )


def solution(mesh):
    return jax.shard_map(
        per_device,
        mesh=mesh,
        in_specs=(
            P(("replica", "fsdp"), None),
            P(("replica", "fsdp"), None),
            P("fsdp"),
            P("fsdp", None),
            P("fsdp", None),
            P("fsdp"),
            P("fsdp", None),
            P(None, "fsdp"),
            P(("replica", "fsdp"), None),
        ),
        out_specs=(
            P(("replica", "fsdp"), None),
            P(("replica", "fsdp"), None),
            P("fsdp"),
            P("fsdp", None),
            P("fsdp", None),
            P("fsdp"),
            P("fsdp", None),
            P(None, "fsdp"),
        ),
        check_vma=False,
    )
```

```python
import jax
import jax.numpy as jnp
from jax import lax
from jax.experimental import pallas as pl
from jax.experimental.pallas import tpu as pltpu
from jax.sharding import PartitionSpec as P

HEAD = 64


NORM_EPS = 1e-05
ROPE_BASE = 160000.0
MASK_FILL = -1000000000.0


def slot_layout(length_pairs, slot_count):
    slot_index = jnp.arange(slot_count, dtype=jnp.int32)[None, :]
    first_length = length_pairs[:, 0:1]
    both_lengths = first_length + length_pairs[:, 1:2]
    segment = jnp.where(
        slot_index < first_length, 0, jnp.where(slot_index < both_lengths, 1, 2)
    ).astype(jnp.int32)
    begin = jnp.where(segment == 0, 0, jnp.where(segment == 1, first_length, both_lengths))
    return (segment, slot_index - begin)


def rope_tables(positions, head_size):
    half_size = head_size // 2
    frequency = ROPE_BASE ** (-(jnp.arange(half_size, dtype=jnp.float32) * 2.0) / head_size)
    angles = positions.astype(jnp.float32)[:, None] * frequency[None, :]
    return (jnp.cos(angles), jnp.sin(angles))


CORE, ALONG_X, ALONG_Y = 1, 2, 4
F32, BF16 = jnp.float32, jnp.bfloat16
VMEM = pl.BlockSpec(memory_space=pltpu.VMEM)
LANES = 128
STEP = 384


def run_kernel(body, name, outs, scratch, operands, microseconds, scalars=0):
    smem = pl.BlockSpec(memory_space=pltpu.SMEM)
    return pl.pallas_call(
        body,
        out_shape=[jax.ShapeDtypeStruct(shape, kind) for shape, kind in outs],
        in_specs=[smem] * scalars + [VMEM] * (len(operands) - scalars),
        out_specs=[VMEM] * len(outs),
        scratch_shapes=scratch,
        compiler_params=pltpu.CompilerParams(vmem_limit_bytes=24 * 2**20),
        cost_estimate=pl.CostEstimate(
            flops=int(microseconds * 1e9), bytes_accessed=0, transcendentals=0
        ),
        name=name,
    )(*operands)


def swap(values, mask):
    return lax.ppermute(values, "fsdp", [(i, i ^ mask) for i in range(8)])


def after(values, *earlier):
    return lax.optimization_barrier((values, earlier))[0]


def gather_first(own):
    return [own, swap(own, ALONG_X), swap(own, ALONG_Y), swap(own, CORE)]


def gather_second(own, from_x, from_y):
    half = own.shape[0] // 2
    return [swap(from_y[:half], ALONG_X), swap(from_x[half:], ALONG_Y)]


def gather_third(first, second):
    own, from_x, from_y, own_core = first
    return [own, from_x, from_y, *second, own_core] + [
        swap(piece, CORE) for piece in (from_x, from_y, *second)
    ]


PIECE_PLACES = [
    (mask | core, first)
    for core in (0, CORE)
    for mask, first in ((0, 0), (ALONG_X, 0), (ALONG_Y, 0), (6, 0), (6, 1))
]


def gathered_whole(own):
    return [lax.all_gather(own, "fsdp", axis=0, tiled=True)]


def lay_out(pieces, targets):
    if len(pieces) == 1:
        places = [(0, 0)]
        me, own_rows = 0, pieces[0].shape[0]
    else:
        places = PIECE_PLACES
        me, own_rows = lax.axis_index("fsdp"), pieces[0].shape[0]
    for piece, (mask, first) in zip(pieces, places):
        rows = piece.shape[0]
        start = (me ^ mask) * own_rows + first * (own_rows // 2)
        start = 0 if len(pieces) == 1 else pl.multiple_of(start, own_rows // 2)
        lane = 0
        for target in targets:
            width = target.shape[1]
            target[pl.ds(start, rows), :] = piece[:, lane : lane + width]
            lane += width


LEAVING = [(6, 0), (ALONG_X, 0), (6, 1), (ALONG_Y, 1), (ALONG_X, 1), (ALONG_Y, 0), (0, 0), (0, 1)]


def pick_rows(values, turned, picked):
    if picked is None:
        turned[...] = values.astype(F32).T.astype(BF16)
        return
    half = turned.shape[0] // 16
    me = lax.axis_index("fsdp")
    turned[...] = values.astype(F32).T.astype(BF16)
    for core in (0, CORE):
        for at, (mask, first) in enumerate(LEAVING):
            start = pl.multiple_of((me ^ (mask | core)) * (2 * half) + first * half, half)
            picked[pl.ds((core * 8 + at) * half, half), :] = turned[pl.ds(start, half), :]


def write_grad(lhs, columns, outs, base=0):
    width = columns.shape[1]
    for lane in range(0, width, STEP):
        product = jnp.dot(
            lhs[...], columns[:, lane : lane + STEP], preferred_element_type=F32
        ).astype(BF16)
        row = 0
        for out in outs:
            out[:, base + lane : base + lane + STEP] = product[row : row + out.shape[0]]
            row += out.shape[0]


def grad_outs(model_width, width):
    if lax.axis_size("fsdp") == 8:
        return [((model_width // 2, width), BF16)] * 2
    return [((model_width, width), BF16)]


def grad_scratch(model_width, slots):
    one = pltpu.VMEM((model_width, slots), BF16)
    return [one, one] if lax.axis_size("fsdp") == 8 else [one]


def write_weight_grad(rows_side, columns, outs, scratch, base=0):
    pick_rows(rows_side, scratch[0], scratch[1] if len(scratch) > 1 else None)
    write_grad(scratch[-1], columns, outs, base)


def dot_nt(a, b):
    return lax.dot_general(a, b, (((1,), (1,)), ((), ())), preferred_element_type=F32)


def dot_tn(a, b):
    return lax.dot_general(a, b, (((0,), (0,)), ((), ())), preferred_element_type=F32)


def dot_nn(a, b):
    return jnp.dot(a, b, preferred_element_type=F32)


def normalised(values):
    mean = jnp.mean(values, -1, keepdims=True)
    centred = values - mean
    scale = lax.rsqrt(jnp.mean(centred * centred, -1, keepdims=True) + NORM_EPS)
    return centred * scale, scale


def norm_back(grad, xhat, scale, gain):
    scaled = grad * gain
    mean = jnp.mean(scaled, -1, keepdims=True)
    along = jnp.mean(scaled * xhat, -1, keepdims=True)
    return scale * (scaled - mean - xhat * along)


def turn_halves(block, cosine, sine):
    lane = lax.broadcasted_iota(jnp.int32, block.shape, 1)
    low_half = (lane % HEAD) < HEAD // 2
    other = jnp.where(
        low_half,
        pltpu.roll(block, LANES - HEAD // 2, 1),
        pltpu.roll(block, HEAD // 2, 1),
    )
    return block * cosine + other * sine


def head_lanes(shape, head):
    lane = lax.broadcasted_iota(jnp.int32, shape, 1)
    return (lane // HEAD) == head


def only(values, head):
    return jnp.where(head_lanes(values.shape, head), values, jnp.zeros_like(values))


def attention_forward(lengths, tokens, cosine, sine, pieces, qkv_width, out_width):
    slots, model_width = tokens.shape
    count = len(pieces)

    def body(*refs):
        lengths_ref, tokens_ref, cosine_ref, sine_ref = refs[:4]
        piece_refs = refs[4 : 4 + count]
        (h1_ref, q_ref, k_ref, v_ref, probs_ref, context_ref, middle_ref, h2_ref, w_qkv, w_out,
         gain_rows, gain_columns, joined) = refs[4 + count :]
        lay_out(piece_refs, [w_qkv, w_out, gain_columns])
        gain_rows[...] = gain_columns[...].astype(F32).T[:8]
        inputs = tokens_ref[...].astype(F32)
        h1_ref[...] = (normalised(inputs)[0] * gain_rows[0:1, :]).astype(BF16)
        for lane in range(0, qkv_width, model_width):
            joined[:, lane : lane + model_width] = dot_nn(
                h1_ref[...], w_qkv[:, lane : lane + model_width]
            )
        first = lengths_ref[0, 0]
        both = first + lengths_ref[0, 1]

        def segment(axis):
            slot = lax.broadcasted_iota(jnp.int32, (slots, slots), axis)
            return (slot >= first).astype(jnp.int32) + (slot >= both).astype(jnp.int32)

        allowed = segment(0) == segment(1)
        cosine_rows, sine_rows = cosine_ref[...], sine_ref[...]
        for lane in range(0, model_width, LANES):
            block = slice(lane, lane + LANES)

            def rope(offset):
                raw = joined[:, offset + lane : offset + lane + LANES]
                return turn_halves(raw, cosine_rows, sine_rows)

            query = (rope(0) * HEAD ** (-0.5)).astype(BF16)
            key = rope(model_width).astype(BF16)
            value = joined[:, 2 * model_width + lane : 2 * model_width + lane + LANES].astype(BF16)
            q_ref[:, block] = query
            k_ref[:, block] = key
            v_ref[:, block] = value
            context = None
            for head in range(2):
                scores = jnp.where(allowed, dot_nt(only(query, head), key), MASK_FILL)
                exponent = jnp.exp(scores - jnp.max(scores, -1, keepdims=True))
                total = jnp.sum(exponent, -1, keepdims=True)
                probs = (exponent * (1.0 / total)).astype(BF16)
                probs_ref[lane // HEAD + head] = probs
                part = dot_nn(probs, only(value, head))
                context = part if context is None else context + part
            context_ref[:, block] = context.astype(BF16)
        middle = inputs + dot_nn(context_ref[...], w_out[...])
        middle_ref[...] = middle
        h2_ref[...] = (normalised(middle)[0] * gain_rows[1:2, :]).astype(BF16)

    wide = (slots, model_width)
    return run_kernel(
        body,
        "attention_forward",
        [(wide, BF16)] * 4
        + [((model_width // HEAD, slots, slots), BF16), (wide, BF16), (wide, F32), (wide, BF16)]
        + [((model_width, qkv_width), BF16), ((model_width, out_width), BF16)]
        + [((8, model_width), F32)],
        [pltpu.VMEM((model_width, LANES), BF16), pltpu.VMEM((slots, qkv_width), F32)],
        [lengths, tokens, cosine, sine, *pieces],
        microseconds=11,
        scalars=1,
    )


ERF_UP = (0.00022905065861350646, 0.0034082910107109506, 0.050955695062380861,
          0.18520832239976145, 1.128379143519084)
ERF_DOWN = (-1.1791602954361697e-7, 0.000023547966471313185, 0.0010179625278914885,
            0.014070470171167667, 0.11098505178285362, 0.49746925110067538, 1.0)


def erf(values):
    values = jnp.clip(values, -3.832506856900711, 3.832506856900711)
    square = values * values
    up = jnp.full_like(values, ERF_UP[0])
    for term in ERF_UP[1:]:
        up = up * square + term
    down = jnp.full_like(values, ERF_DOWN[0])
    for term in ERF_DOWN[1:]:
        down = down * square + term
    return values * up / down


def feed_forward(h2, cotangent, pieces, in_width, ff_width):
    slots, model_width = h2.shape
    count = len(pieces)
    outs = grad_outs(model_width, ff_width)
    scratch = grad_scratch(model_width, slots)

    def body(*refs):
        h2_ref, cotangent_ref = refs[:2]
        piece_refs = refs[2 : 2 + count]
        mixed_ref, grad_hidden_ref, w_in, w_down_t = refs[2 + count : 6 + count]
        grad_refs = refs[6 + count : 6 + count + len(outs)]
        turning = refs[6 + count + len(outs) :]
        lay_out(piece_refs, [w_in, w_down_t])
        grad_out = cotangent_ref[...].astype(BF16)
        for lane in range(0, ff_width, STEP):
            here, there = slice(lane, lane + STEP), slice(ff_width + lane, ff_width + lane + STEP)
            raw = dot_nn(h2_ref[...], w_in[:, here])
            gate = dot_nn(h2_ref[...], w_in[:, there])
            grad_mixed = dot_nn(grad_out, w_down_t[:, here])
            below = 0.5 * (1.0 + erf(raw * 0.7071067811865476))
            bell = jnp.exp(raw * raw * -0.5) * 0.3989422804014327
            active = raw * below
            mixed_ref[:, here] = (active * gate).astype(BF16)
            grad_hidden_ref[:, here] = (grad_mixed * gate * (below + raw * bell)).astype(BF16)
            grad_hidden_ref[:, there] = (grad_mixed * active).astype(BF16)
        write_weight_grad(cotangent_ref[...], mixed_ref, grad_refs, turning)

    results = run_kernel(
        body,
        "feed_forward",
        [((slots, ff_width), BF16), ((slots, in_width), BF16)]
        + [((model_width, in_width), BF16), ((model_width, ff_width), BF16)]
        + outs,
        scratch,
        [h2, cotangent, *pieces],
        microseconds=8,
    )
    return results[:4], results[4:]


def weight_grad(rows_side, columns_side):
    slots, model_width = rows_side.shape
    outs = grad_outs(model_width, columns_side.shape[1])

    def body(rows_ref, columns_ref, *refs):
        write_weight_grad(rows_ref[...], columns_ref, refs[: len(outs)], refs[len(outs) :])

    return run_kernel(
        body,
        "weight_grad",
        outs,
        grad_scratch(model_width, slots),
        [rows_side, columns_side],
        microseconds=1.5,
    )


def middle_backward(grad_hidden, w_in, middle, gains, cotangent, w_out):
    def body(grad_hidden_ref, w_in_ref, middle_ref, gains_ref, cotangent_ref, w_out_ref,
             grad_middle_ref, grad_context_ref):
        grad_h2 = dot_nt(grad_hidden_ref[...], w_in_ref[...])
        xhat, scale = normalised(middle_ref[...])
        grad_middle = cotangent_ref[...] + norm_back(grad_h2, xhat, scale, gains_ref[1:2, :])
        grad_middle_ref[...] = grad_middle
        grad_context_ref[...] = dot_nt(grad_middle.astype(BF16), w_out_ref[...]).astype(BF16)

    return run_kernel(
        body,
        "middle_backward",
        [(middle.shape, F32), (middle.shape, BF16)],
        [],
        [grad_hidden, w_in, middle, gains, cotangent, w_out],
        microseconds=5,
    )


def attention_backward(
    query, key, value, probs, context, grad_context, cosine, sine, h1, grad_middle
):
    slots, model_width = query.shape
    outs = grad_outs(model_width, 2 * model_width)
    scratch = grad_scratch(model_width, slots)

    def body(q_ref, k_ref, v_ref, probs_ref, context_ref, grad_context_ref, cosine_ref, sine_ref,
             h1_ref, grad_middle_ref, joined_ref, *refs):
        cosine_rows, sine_rows = cosine_ref[...], -sine_ref[...]
        for lane in range(0, model_width, LANES):
            block = slice(lane, lane + LANES)
            query, key, value = q_ref[:, block], k_ref[:, block], v_ref[:, block]
            grad = grad_context_ref[:, block]
            product = grad.astype(F32) * context_ref[:, block].astype(F32)
            grad_query = grad_key = grad_value = 0.0
            for head in range(2):
                here = probs_ref[lane // HEAD + head]
                inner = jnp.sum(only(product, head), -1, keepdims=True)
                grad_probs = dot_nt(only(grad, head), value)
                grad_scores = (here.astype(F32) * (grad_probs - inner)).astype(BF16)
                grad_value += dot_tn(only(grad, head), here)
                grad_query += dot_nn(grad_scores, only(key, head))
                grad_key += dot_tn(only(query, head), grad_scores)
            grad_query = turn_halves(grad_query * HEAD ** (-0.5), cosine_rows, sine_rows)
            grad_key = turn_halves(grad_key.T, cosine_rows, sine_rows)
            joined_ref[:, block] = grad_query.astype(BF16)
            joined_ref[:, model_width + lane : model_width + lane + LANES] = grad_key.astype(BF16)
            joined_ref[:, 2 * model_width + lane : 2 * model_width + lane + LANES] = (
                grad_value.T.astype(BF16)
            )
        count = len(outs)
        first, second = refs[:count], refs[count : 2 * count]
        turned_context = refs[2 * count : 2 * count + len(scratch)]
        turned, narrow = refs[2 * count + len(scratch) : -1], refs[-1]
        narrow[...] = grad_middle_ref[...].astype(BF16)
        write_weight_grad(context_ref[...], narrow, first, turned_context, 0)
        write_weight_grad(
            h1_ref[...], joined_ref.at[:, 2 * model_width :], first, turned, model_width
        )
        write_grad(turned[-1], joined_ref.at[:, : 2 * model_width], second, 0)

    results = run_kernel(
        body,
        "attention_backward",
        [((slots, 3 * model_width), BF16)] + outs + outs,
        scratch * 2 + [pltpu.VMEM((slots, model_width), BF16)],
        [query, key, value, probs, context, grad_context, cosine, sine, h1, grad_middle],
        microseconds=6,
    )
    count = len(outs)
    return results[0], results[1 : 1 + count], results[1 + count :]


def layer_output(middle, mixed, w_down_t):
    def body(middle_ref, mixed_ref, w_down_ref, output_ref):
        output = middle_ref[...] + dot_nt(mixed_ref[...], w_down_ref[...])
        output_ref[...] = output.astype(BF16)

    outs = [(middle.shape, BF16)]
    operands = [middle, mixed, w_down_t]
    return run_kernel(body, "layer_output", outs, [], operands, microseconds=2)[0]


def input_grad(tokens, grad_joined, w_qkv, grad_middle, gains):
    def body(tokens_ref, joined_ref, w_qkv_ref, grad_middle_ref, gains_ref, grad_ref):
        grad_h1 = dot_nt(joined_ref[...], w_qkv_ref[...])
        xhat, scale = normalised(tokens_ref[...].astype(F32))
        grad_ref[...] = grad_middle_ref[...] + norm_back(grad_h1, xhat, scale, gains_ref[0:1, :])

    outs = [(tokens.shape, F32)]
    operands = [tokens, grad_joined, w_qkv, grad_middle, gains]
    return run_kernel(body, "input_grad", outs, [], operands, microseconds=3)[0]


def add(*parts):
    return sum(part.astype(F32) for part in parts)


class Steps:
    def hold(self, earlier, *names):
        for name, held in zip(names, after([getattr(self, n) for n in names], *earlier)):
            setattr(self, name, held)


class ShardSum(Steps):
    def __init__(self, parts):
        self.keep, send = parts
        self.half = self.keep.shape[0] // 8
        self.other = swap(send, CORE)

    def chip(self, first, count, *more):
        rows = slice(first * self.half, (first + count) * self.half)
        return add(self.keep[rows], self.other[rows], *more)

    def ready_one(self):
        self.to_x = self.chip(0, 2).astype(BF16)
        self.to_y = self.chip(2, 2).astype(BF16)
        return self.to_x, self.to_y

    def send_one(self):
        self.by_x, self.by_y = swap(self.to_x, ALONG_X), swap(self.to_y, ALONG_Y)

    def ready_two(self):
        self.late_x = self.chip(4, 1, self.by_y[: self.half]).astype(BF16)
        self.late_y = self.chip(5, 1, self.by_x[: self.half]).astype(BF16)
        return self.late_x, self.late_y

    def send_two(self):
        self.from_x, self.from_y = swap(self.late_x, ALONG_X), swap(self.late_y, ALONG_Y)

    def result(self):
        first = self.chip(6, 1, self.by_x[self.half :], self.from_y)
        second = self.chip(7, 1, self.by_y[self.half :], self.from_x)
        return first, second


class CopiesSum(Steps):
    def __init__(self, first, second):
        self.odd = lax.axis_index("replica") % 2 == 1
        self.mine = jnp.where(self.odd, second, first)
        self.theirs = jnp.where(self.odd, first, second).astype(BF16)

    def swap(self, values, mask):
        return lax.ppermute(values, "replica", [(i, i ^ mask) for i in range(4)])

    def send_one(self):
        self.near = self.swap(self.theirs, 1)

    def ready_two(self):
        self.pair = add(self.mine, self.near).astype(BF16)
        return self.pair

    def send_two(self):
        self.far = self.swap(self.pair, 2)

    def send_three(self):
        self.total = add(self.pair, self.far).astype(BF16)
        self.back = self.swap(self.total, 1)


def place_halves(total_ref, back_ref, out_ref, columns=slice(None)):
    half = total_ref.shape[0]
    odd = lax.rem(lax.axis_index("replica"), 2)
    for ref, at in ((total_ref, odd), (back_ref, 1 - odd)):
        rows = pl.ds(pl.multiple_of(at * half, half), half)
        out_ref[rows, :] = ref[:, columns].astype(F32)


def write_gain_grad(weight, weight_sum, gain_ref, out_ref):
    column = jnp.sum(weight.astype(F32) * weight_sum, 1, keepdims=True)
    row = jnp.broadcast_to(column, (column.shape[0], LANES)).T[:1]
    out_ref[...] = row / gain_ref[...].astype(F32)


def down_result(group):
    half, width = group.total.shape

    def body(total_ref, back_ref, out_ref):
        place_halves(total_ref, back_ref, out_ref)

    outs = [((2 * half, width), F32)]
    return run_kernel(body, "down_result", outs, [], [group.total, group.back], microseconds=1)[0]


def in_result(group, weight, gain):
    half, width = group.total.shape

    def body(total_ref, back_ref, weight_ref, gain_ref, out_ref, gain_out_ref):
        place_halves(total_ref, back_ref, out_ref)
        write_gain_grad(weight_ref[...], out_ref[...], gain_ref, gain_out_ref)

    outs = [((2 * half, width), F32), ((1, 2 * half), F32)]
    operands = [group.total, group.back, weight, gain[None]]
    result, gain_result = run_kernel(body, "in_result", outs, [], operands, microseconds=1)
    return result, gain_result[0]


def attention_result(early, late, weight, gain):
    half, width = early.total.shape
    each = width // 2

    def body(early_total, early_back, late_total, late_back, weight_ref, gain_ref,
             qkv_ref, out_ref, gain_out_ref):
        place_halves(late_total, late_back, qkv_ref.at[:, :width])
        place_halves(early_total, early_back, qkv_ref.at[:, width:], slice(each, width))
        place_halves(early_total, early_back, out_ref, slice(0, each))
        write_gain_grad(weight_ref[...], qkv_ref[...], gain_ref, gain_out_ref)

    outs = [((2 * half, 3 * each), F32), ((2 * half, each), F32), ((1, 2 * half), F32)]
    operands = [early.total, early.back, late.total, late.back, weight, gain[None]]
    qkv, out, gain_result = run_kernel(
        body, "attention_result", outs, [], operands, microseconds=1
    )
    return qkv, out, gain_result[0]


def whole_sum(part):
    shard = lax.psum_scatter(part, "fsdp", scatter_dimension=0, tiled=True)
    return lax.psum(shard, "replica").astype(F32)


def per_device(
    tokens,
    seq_lengths,
    norm1_gain,
    qkv_weight,
    out_weight,
    norm2_gain,
    in_weight,
    down_weight,
    cotangent,
):
    slot_count = tokens.shape[0]
    qkv_width, out_width = qkv_weight.shape[1], out_weight.shape[1]
    in_width, ff_width = in_weight.shape[1], down_weight.shape[0]
    gain_columns = jnp.pad(jnp.stack([norm1_gain, norm2_gain], 1), ((0, 0), (0, LANES - 2)))
    attn_own = jnp.concatenate([qkv_weight, out_weight, gain_columns], 1)
    mlp_own = jnp.concatenate([in_weight, down_weight.T], 1)
    exchange = lax.axis_size("fsdp") == 8 and lax.axis_size("replica") == 4
    if exchange:
        attn_first = gather_first(attn_own)
        attn_second = gather_second(*attn_first[:3])
        attn_pieces = gather_third(attn_first, attn_second)
        mlp_own = after(mlp_own, *attn_second)
        mlp_first = gather_first(mlp_own)
    else:
        attn_pieces, mlp_pieces = gathered_whole(attn_own), gathered_whole(mlp_own)
    positions = slot_layout(seq_lengths, slot_count)[1][0]
    cosine, sine = rope_tables(positions, HEAD)
    cosine = jnp.concatenate([cosine] * 4, 1)
    sine = jnp.concatenate([-sine, sine, -sine, sine], 1)

    (h1, query, key, value, probs, context, middle, h2, w_qkv, w_out, gains) = attention_forward(
        seq_lengths, tokens, cosine, sine, attn_pieces, qkv_width, out_width
    )
    if exchange:
        mlp_first = after(mlp_first, h2)
        mlp_pieces = gather_third(mlp_first, gather_second(*mlp_first[:3]))
    (mixed, grad_hidden, w_in, w_down_t), down_parts = feed_forward(
        h2, cotangent, mlp_pieces, in_width, ff_width
    )
    if exchange:
        down = ShardSum(down_parts)
    in_parts = weight_grad(h2, grad_hidden)
    if exchange:
        into = ShardSum(in_parts)
        down.hold(in_parts, "other")
        grad_hidden = after(grad_hidden, *down.ready_one())
        down.send_one()
    grad_middle, grad_context = middle_backward(
        grad_hidden, w_in, middle, gains, cotangent, w_out
    )
    if exchange:
        into.hold([grad_context], "other")
        down.hold([grad_context], "by_x", "by_y")
        grad_context = after(grad_context, *into.ready_one(), *down.ready_two())
        into.send_one()
        down.send_two()
    grad_joined, early_parts, late_parts = attention_backward(
        query, key, value, probs, context, grad_context, cosine, sine, h1, grad_middle
    )
    if exchange:
        early, late = ShardSum(early_parts), ShardSum(late_parts)
        down.hold([grad_joined], "from_x", "from_y")
        down_copies = CopiesSum(*down.result())
        mixed = after(mixed, *early.ready_one(), down_copies.theirs)
        down_copies.send_one()
        early.send_one()
    output = layer_output(middle, mixed, w_down_t)
    if exchange:
        into.hold([output], "by_x", "by_y")
        down_copies.hold([output], "near")
        late.hold([output], "other")
        grad_middle = after(grad_middle, *into.ready_two(), *late.ready_one(), down_copies.ready_two())
        into.send_two()
        late.send_one()
        down_copies.send_two()
    grad_tokens = input_grad(tokens, grad_joined, w_qkv, grad_middle, gains)
    if exchange:
        early.hold([grad_tokens], "by_x", "by_y")
        into.hold([grad_tokens], "from_x", "from_y")
        late.hold([grad_tokens], "by_x", "by_y")
        early.ready_two()
        early.send_two()
        into_copies = CopiesSum(*into.result())
        into_copies.send_one()
        late.ready_two()
        late.send_two()
        down_copies.send_three()
        into_copies.ready_two()
        into_copies.send_two()
        into_copies.send_three()
        early_copies = CopiesSum(*early.result())
        late_copies = CopiesSum(*late.result())
        for group in (early_copies, late_copies):
            group.send_one()
            group.ready_two()
            group.send_two()
            group.send_three()
        grad_down = down_result(down_copies)
        grad_in, grad_norm2 = in_result(into_copies, in_weight, norm2_gain)
        grad_qkv, grad_out, grad_norm1 = attention_result(
            early_copies, late_copies, qkv_weight, norm1_gain
        )
    else:
        grad_down, grad_in = whole_sum(down_parts[0]), whole_sum(in_parts[0])
        early_sum, late_sum = whole_sum(early_parts[0]), whole_sum(late_parts[0])
        grad_out, grad_values = early_sum[:, :out_width], early_sum[:, out_width:]
        grad_qkv = jnp.concatenate([late_sum, grad_values], 1)

        def gain_grad(weight, weight_sum, gain):
            return jnp.sum(weight.astype(F32) * weight_sum, 1) / gain.astype(F32)

        grad_norm1 = gain_grad(qkv_weight, grad_qkv, norm1_gain)
        grad_norm2 = gain_grad(in_weight, grad_in, norm2_gain)

    return (
        output,
        grad_tokens,
        grad_norm1,
        grad_qkv,
        grad_out,
        grad_norm2,
        grad_in,
        grad_down.T,
    )


def solution(mesh):
    return jax.shard_map(
        per_device,
        mesh=mesh,
        in_specs=(
            P(("replica", "fsdp"), None),
            P(("replica", "fsdp"), None),
            P("fsdp"),
            P("fsdp", None),
            P("fsdp", None),
            P("fsdp"),
            P("fsdp", None),
            P(None, "fsdp"),
            P(("replica", "fsdp"), None),
        ),
        out_specs=(
            P(("replica", "fsdp"), None),
            P(("replica", "fsdp"), None),
            P("fsdp"),
            P("fsdp", None),
            P("fsdp", None),
            P("fsdp"),
            P("fsdp", None),
            P(None, "fsdp"),
        ),
        check_vma=False,
    )
```
